512 devices in a mesh: stream: 32 (over x, y, core), ctx: 16 (over z).
Axes of the slice: x: 4, y: 4, z: 16, core: 2. Of those that a mesh axis runs over, the one named last changes fastest.
Arguments:
- new_queries: bfloat16 [4096, 8192], P('stream', 'ctx'), may hold values from -8 to 8
- new_keys: bfloat16 [4096, 1024], P('stream'), may hold values from -8 to 8
- new_values: bfloat16 [4096, 1024], P('stream'), may hold values from -6 to 6
- cache_keys: bfloat16 [131072, 1024], P(('stream', 'ctx')), may hold values from -8 to 8
- cache_values: bfloat16 [131072, 1024], P(('stream', 'ctx')), may hold values from -6 to 6
- new_counts: int32 [32], replicated, may hold values from 16 to 128, as said below
- ctx_lengths: int32 [32], replicated, may hold values from 2 to 4096, as said below
- offloads: int32 [8, 4], replicated, may hold values from 0 to 31, as said below
Outputs:
- mixed_rows: bfloat16 [4096, 8192], P('stream', 'ctx')
- hosted: bfloat16 [2048, 8192], P('stream', 'ctx')
The draws below stay inside these ranges and needn't reach their ends.
Inputs may be any that keep to these rules, and one draw needn't show every extreme that they name: `new_counts`: some stream has all 128 rows live; every source stream of offloads has all 128 rows live. `ctx_lengths`: some stream uses all 4096 cached positions. `offloads`: the 8 sources are distinct streams and so are the 8 destinations; no stream is both. A run's blocks are 1 to 2, some run has 2, and first + blocks <= 4.
All inputs are finite; a program needn't handle non-finite values.
Results may differ from the reference program's by a relative error of at most 0.0095.
Values may be sent and summed in bfloat16 or wider, within the bound.
A program may use at most 64 MiB of HBM per device.

```python
import math
import jax
import jax.numpy as jnp
from jax import lax

HEADS = 64
KV = 8
HD = 128
BLK = 32
NB = 4
CTX_DEV = 256
CAP_BLK = 2
STREAMS = 32
OFFLOADS = 8
NEW = 128
CTX = 4096
CAP = 64
N_CTX = 16


def offload_plan(key):
    half = STREAMS // 2
    offsets = jnp.array([0, half, half + 1, half + 2])
    slot = jax.random.randint(jax.random.fold_in(key, 20), (), 0, 4)
    base = (STREAMS - 1 - offsets[slot]) % STREAMS
    fixed_ids = (base + offsets) % STREAMS
    order = jax.random.permutation(jax.random.fold_in(key, 21), STREAMS)
    position = jnp.argsort(order)
    stream_ids = jnp.arange(STREAMS)
    is_fixed = jnp.any(stream_ids[:, None] == fixed_ids[None, :], axis=1)
    ranking = position + STREAMS * is_fixed.astype(jnp.int32)
    rest = jnp.argsort(ranking, stable=True)
    extra = OFFLOADS - 2
    sources = jnp.concatenate([fixed_ids[1:3], rest[:extra]])
    targets = jnp.concatenate([fixed_ids[0:1], fixed_ids[3:4], rest[extra:2 * extra]])
    spans = jax.random.randint(jax.random.fold_in(key, 22), (OFFLOADS,), 1, CAP_BLK + 1)
    spans = spans.at[0].set(CAP_BLK)
    starts = jax.random.randint(jax.random.fold_in(key, 23), (OFFLOADS,), 0, NB - spans + 1)
    starts = starts.at[0].set(0)
    counts = jax.random.randint(jax.random.fold_in(key, 24), (STREAMS,), BLK // 2, NEW + 1)
    counts = counts.at[sources].set(NEW)
    return (sources, targets, starts, spans, counts)


def draw_new_queries(key, part):
    key = jax.random.fold_in(key, 1)
    drawn = jax.random.truncated_normal(key, -5.0, 5.0, (STREAMS, NEW, HEADS, HD))
    return drawn.reshape(STREAMS * NEW, HEADS * HD).astype(jnp.bfloat16)


def draw_new_keys(key, part):
    key = jax.random.fold_in(key, 2)
    drawn = jax.random.truncated_normal(key, -5.0, 5.0, (STREAMS, NEW, KV, HD))
    return drawn.reshape(STREAMS * NEW, KV * HD).astype(jnp.bfloat16)


def draw_cache_keys(key, part):
    key = jax.random.fold_in(key, 3)
    drawn = jax.random.truncated_normal(key, -5.0, 5.0, (STREAMS, CTX, KV, HD))
    return drawn.reshape(STREAMS * CTX, KV * HD).astype(jnp.bfloat16)


def draw_new_counts(key, part):
    sources, targets, starts, spans, counts = offload_plan(key)
    return counts.astype(jnp.int32)


def draw_ctx_lengths(key, part):
    key = jax.random.fold_in(key, 5)
    lengths = jax.random.randint(jax.random.fold_in(key, 1), (STREAMS,), 2, CTX + 1)
    fullest = jax.random.randint(jax.random.fold_in(key, 2), (), 0, STREAMS)
    return lengths.at[fullest].set(CTX).astype(jnp.int32)


def draw_offloads(key, part):
    sources, targets, starts, spans, counts = offload_plan(key)
    return jnp.stack([sources, targets, starts, spans], axis=1).astype(jnp.int32)


def shard_levels(stream_key, dims, pieces, least, top_value):
    gain, own = 1.0, jax.random.fold_in(stream_key, 6)
    for dim, blocks in pieces:
        draws = jnp.exp(jax.random.uniform(jax.random.fold_in(own, dim), (blocks,), jnp.float32, least / len(pieces), top_value / len(pieces)))
        gain = gain * jnp.repeat(draws, dims[dim] // blocks).reshape([-1 if axis == dim else 1 for axis in range(len(dims))])
    return gain


def scatter_about(own_key, extent, spread, limit, split=(), held_as=jnp.bfloat16):
    result = jax.random.normal(own_key, extent, jnp.float32) * spread
    if len(split) > 0:
        result = shard_levels(own_key, extent, split, -0.22, 0.18) * result
    return jnp.clip(result, min=-limit, max=limit).astype(held_as)


def setup_inputs(seed: int = 0) -> dict:
    arg_keys = jax.random.split(jax.random.key(seed), 9)
    return {
        "new_queries": draw_new_queries(jax.random.fold_in(arg_keys[8], 71), 0),
        "new_keys": draw_new_keys(jax.random.fold_in(arg_keys[8], 71), 0),
        "new_values": scatter_about(arg_keys[2], (STREAMS * NEW, KV * HD), 1.0, 6.0, ((0, 32),)),
        "cache_keys": draw_cache_keys(jax.random.fold_in(arg_keys[8], 71), 0),
        "cache_values": scatter_about(arg_keys[4], (STREAMS * CTX, KV * HD), 1.0, 6.0, ((0, 512),)),
        "new_counts": draw_new_counts(jax.random.fold_in(arg_keys[8], 71), 0),
        "ctx_lengths": draw_ctx_lengths(jax.random.fold_in(arg_keys[8], 71), 0),
        "offloads": draw_offloads(jax.random.fold_in(arg_keys[8], 71), 0),
    }


NEG = -1e+30

def partial_softmax(queries, key_rows, value_rows, visible):
    scale = 1.0 / math.sqrt(HD)
    scores = jnp.einsum('rkge,pke->rkgp', queries.astype(jnp.float32), key_rows.astype(jnp.float32)) * scale
    allowed = visible[:, None, None, :]
    scores = jnp.where(allowed, scores, NEG)
    maxima = lax.optimization_barrier(jnp.max(scores, axis=-1))
    weights = jnp.where(allowed, jnp.exp(scores - maxima[..., None]), 0.0)
    totals = lax.optimization_barrier(jnp.sum(weights, axis=-1))
    rounded = lax.optimization_barrier(weights.astype(jnp.bfloat16)).astype(jnp.float32)
    weighted = jnp.einsum('rkgp,pke->rkge', rounded, value_rows.astype(jnp.float32))
    return (weighted / jnp.maximum(totals, 1.0)[..., None], maxima, totals)

def merge_blocks(partials, maxima, totals):
    largest = lax.optimization_barrier(jnp.max(maxima, axis=0))
    scaled = totals * jnp.exp(maxima - largest)
    summed = lax.optimization_barrier(jnp.sum(scaled, axis=0))
    combined = lax.optimization_barrier(jnp.sum(scaled[..., None] * partials.astype(jnp.float32), axis=0))
    return ((combined / summed[..., None]).astype(jnp.bfloat16), largest, summed)

def finish(cache_out, largest, summed, own_out, own_max, own_total):
    highest = jnp.maximum(largest, own_max)
    first_weight = summed * jnp.exp(largest - highest)
    second_weight = own_total * jnp.exp(own_max - highest)
    mixed = first_weight[..., None] * cache_out.astype(jnp.float32) + second_weight[..., None] * own_out
    return (mixed / (first_weight + second_weight)[..., None]).astype(jnp.bfloat16)

def stream_rows(operands):
    queries, new_k, new_v, cached_keys, cached_values, length = operands

    def one_block(block_id):
        key_rows = lax.dynamic_index_in_dim(cached_keys, block_id, 0, keepdims=False)
        value_rows = lax.dynamic_index_in_dim(cached_values, block_id, 0, keepdims=False)
        positions = block_id * CTX_DEV + jnp.arange(CTX_DEV).astype(jnp.int32)
        visible = jnp.broadcast_to((positions < length)[None, :], (NEW, CTX_DEV))
        partial_value, maxima, totals = partial_softmax(queries, key_rows, value_rows, visible)
        return (partial_value.astype(jnp.bfloat16), maxima, totals)
    partials, maxima, totals = lax.map(one_block, jnp.arange(N_CTX).astype(jnp.int32))
    cache_out, largest, summed = merge_blocks(partials, maxima, totals)
    row_ids = jnp.arange(NEW).astype(jnp.int32)
    causal = row_ids[None, :] <= row_ids[:, None]
    own_out, own_max, own_total = partial_softmax(queries, new_k, new_v, causal)
    return finish(cache_out, largest, summed, own_out, own_max, own_total)

def reference(new_queries, new_keys, new_values, cache_keys, cache_values, new_counts, ctx_lengths, offloads):
    per_kv = HEADS // KV
    queries = new_queries.reshape(STREAMS, NEW, KV, per_kv, HD)
    new_k = new_keys.reshape(STREAMS, NEW, KV, HD)
    new_v = new_values.reshape(STREAMS, NEW, KV, HD)
    cached_keys = cache_keys.reshape(STREAMS, N_CTX, CTX_DEV, KV, HD)
    cached_values = cache_values.reshape(STREAMS, N_CTX, CTX_DEV, KV, HD)
    results = lax.map(stream_rows, (queries, new_k, new_v, cached_keys, cached_values, ctx_lengths))
    results = results.reshape(STREAMS, NEW, HEADS * HD)
    row_ids = jnp.arange(NEW).astype(jnp.int32)
    stream_ids = jnp.arange(STREAMS).astype(jnp.int32)
    sources = offloads[:, 0]
    targets = offloads[:, 1]
    starts = offloads[:, 2] * BLK
    spans = offloads[:, 3] * BLK
    inside = (row_ids[None, None, :] >= starts[:, None, None]) & (row_ids[None, None, :] < (starts + spans)[:, None, None])
    handed = jnp.any((sources[:, None, None] == stream_ids[None, :, None]) & inside, axis=0)
    retained = (row_ids[None, :] < new_counts[:, None]) & jnp.logical_not(handed)
    mixed_rows = jnp.where(retained[..., None], results, 0.0).astype(jnp.bfloat16).reshape(STREAMS * NEW, HEADS * HD)
    padded = jnp.concatenate([results, jnp.zeros((STREAMS, CAP, HEADS * HD), jnp.bfloat16)], axis=1)

    def guest_rows(stream_id):
        wanted = targets == stream_id
        has_guest = jnp.any(wanted)
        guest_source = jnp.sum(jnp.where(wanted, sources, 0)).astype(jnp.int32)
        guest_start = jnp.sum(jnp.where(wanted, starts, 0)).astype(jnp.int32)
        guest_span = jnp.sum(jnp.where(wanted, spans, 0)).astype(jnp.int32)
        chosen = lax.dynamic_index_in_dim(padded, guest_source, 0, keepdims=False)
        taken = lax.dynamic_slice_in_dim(chosen, guest_start, CAP, 0)
        keep_rows = has_guest & (jnp.arange(CAP).astype(jnp.int32) < guest_span)
        return jnp.where(keep_rows[:, None], taken, 0.0).astype(jnp.bfloat16)
    hosted = lax.map(guest_rows, stream_ids).reshape(STREAMS * CAP, HEADS * HD)
    return (mixed_rows, hosted)
```

```python
import functools
import math

import jax
import jax.numpy as jnp
from jax import lax
from jax.experimental import pallas as pl
from jax.experimental.pallas import tpu as pltpu
from jax.sharding import PartitionSpec as P

HEADS = 64
KV = 8
HD = 128
BLK = 32
NEW = 128
CAP = 64
RUNS = 8
N_CTX = 16
N_STREAM = 32
CHIPS = N_STREAM // 2
SIDE = N_CTX // 2
REACH = 3
FAR = SIDE - 1 - REACH
HALF = NEW // 2
QROWS = 4 * HALF
PACK = HD + 16

NEG = -(2.0**100)
LOG2_SCALE = math.log2(math.e) / math.sqrt(HD)
MESH = pl.DeviceIdType.MESH


def merge(first, second):
    acc_a, max_a, tot_a = first
    acc_b, max_b, tot_b = second
    top = jnp.maximum(max_a, max_b)
    scale_a = jnp.exp2(max_a - top)
    scale_b = jnp.exp2(max_b - top)
    return (acc_a * scale_a + acc_b * scale_b, top, tot_a * scale_a + tot_b * scale_b)


def attend(keys, values_t, queries, allowed):
    scores = lax.dot_general(
        keys, queries, (((1,), (1,)), ((), ())), preferred_element_type=jnp.float32
    )
    scores = jnp.where(allowed, scores * LOG2_SCALE, NEG)
    top = jnp.max(scores, axis=0, keepdims=True).astype(jnp.bfloat16).astype(jnp.float32)
    weights = jnp.exp2(scores - top)
    total = jnp.sum(weights, axis=0, keepdims=True)
    acc = jnp.dot(values_t, weights.astype(jnp.bfloat16), preferred_element_type=jnp.float32)
    return acc, top, total


def pack_rows(top, total):
    high = total.astype(jnp.bfloat16).astype(jnp.float32)
    low = total - high
    width = top.shape[1]
    row = lax.broadcasted_iota(jnp.int32, (16, width), 0)
    rows = jnp.where(row == 0, top, jnp.where(row == 1, high, jnp.where(row == 2, low, 0.0)))
    return rows.astype(jnp.bfloat16)


def unpack(packed):
    stats = packed[HD:PACK, :].astype(jnp.float32)
    return packed[:HD, :].astype(jnp.float32), stats[0:1], stats[1:2] + stats[2:3]


def kernel(
    counts_ref, lengths_ref, offloads_ref,
    q_hbm, nk_hbm, nv_hbm, ck_hbm, cv_hbm,
    mixed_ref, hosted_ref,
    q_in, nk, nv, ck, cv, vt, qbuf, kbuf, vbuf, acc_ref, stat_ref, osend, orecv, psend, precv,
    fin_f, run, p1, p3, host,
    in_sem, kv_s, kv_r, q_s, q_r, o_s, o_r, p_s, p_r, p1_s, p1_r, p2_s, p2_r, p3_s, p3_r,
):
    s = lax.axis_index("stream")
    t = lax.axis_index("ctx")
    core = lax.rem(s, 2)
    chip = s // 2
    side = 1 - 2 * lax.rem(t, 2)

    def ring(v):
        return lax.rem(v + 2 * N_CTX, N_CTX)

    def inward(i):
        return side if i % 2 == 0 else -side

    def near(i):
        return ring(t + inward(i) * i)

    def head(i):
        return near(i) // 2

    def columns(i):
        return pl.ds(pl.multiple_of(head(i) * HD, HD), HD)

    own_kv = pl.ds(pl.multiple_of((t // 2) * HD, HD), HD)
    loads = [
        pltpu.make_async_copy(q_hbm, q_in, in_sem.at[0]),
        pltpu.make_async_copy(ck_hbm, ck, in_sem.at[1]),
        pltpu.make_async_copy(cv_hbm, cv, in_sem.at[2]),
        pltpu.make_async_copy(nk_hbm.at[:, own_kv], nk, in_sem.at[3]),
        pltpu.make_async_copy(nv_hbm.at[:, own_kv], nv, in_sem.at[4]),
    ]
    barrier = pltpu.get_barrier_semaphore()
    reach = max(FAR, 1)
    greeted = 0
    for k in range(1, reach + 1):
        for sign in (1, -1):
            pl.semaphore_signal(barrier, inc=1, device_id=(s, ring(t + sign * k)), device_id_type=MESH)
            greeted += 1
    for k in range(1, CHIPS):
        peer = 2 * lax.rem(chip + k, CHIPS) + core
        pl.semaphore_signal(barrier, inc=1, device_id=(peer, t), device_id_type=MESH)
        greeted += 1
    sibling = s + 1 - 2 * core
    pl.semaphore_signal(barrier, inc=1, device_id=(sibling, t), device_id_type=MESH)
    greeted += 1
    for copy in loads:
        copy.start()

    out_first = jnp.int32(0)
    out_span = jnp.int32(0)
    in_span = jnp.int32(0)
    for i in range(RUNS):
        mine = offloads_ref[i, 0] == s
        out_first += jnp.where(mine, offloads_ref[i, 2], 0)
        out_span += jnp.where(mine, offloads_ref[i, 3] * BLK, 0)
        in_span += jnp.where(offloads_ref[i, 1] == s, offloads_ref[i, 3] * BLK, 0)
    count = counts_ref[s]
    length = lengths_ref[s]
    first = jnp.minimum(out_first, 2)
    rest_a = jnp.where(first == 0, 2, 0)
    rest_b = jnp.where(first == 2, 1, 3)
    order = ((first, first + 1), (rest_a, rest_b))
    out_start = out_first * BLK

    loads[0].wait()
    for h in range(2):
        for part in range(2):
            rows = q_in[order[h][part]]
            for n in range(4):
                lo = n * HALF + part * BLK
                qbuf[0, 0, h, lo : lo + BLK, :] = rows[:, n * HD : (n + 1) * HD]
    loads[1].wait()
    loads[2].wait()
    pl.semaphore_wait(barrier, greeted)

    def remote(src, dst, send, recv, device):
        return pltpu.make_async_remote_copy(
            src_ref=src, dst_ref=dst, send_sem=send, recv_sem=recv, device_id=device, device_id_type=MESH
        )

    def kv_copies(i):
        target = (s, ring(t + inward(i) * (i - REACH)))
        slot = i - REACH - 1
        return (
            remote(ck.at[:, columns(i)], kbuf.at[slot], kv_s.at[0, slot], kv_r.at[0, slot], target),
            remote(cv.at[:, columns(i)], vbuf.at[slot], kv_s.at[1, slot], kv_r.at[1, slot], target),
        )

    def q_partner(h):
        return remote(
            qbuf.at[0, 0, h], qbuf.at[0, 1, h], q_s.at[0, 2, h], q_r.at[0, 1, h], (s, ring(t + inward(0)))
        )

    def q_outward(i, o, h):
        return remote(
            qbuf.at[i, o, h], qbuf.at[i + 1, o, h], q_s.at[i, o, h], q_r.at[i + 1, o, h],
            (s, ring(t - inward(i))),
        )

    def q_arrival(i, o, h):
        return q_partner(h) if i == 0 else q_outward(i - 1, o, h)

    def out_inward(i, h):
        return remote(
            osend.at[i - 1, h], orecv.at[i - 1, h], o_s.at[i - 1, h], o_r.at[i - 1, h],
            (s, ring(t + inward(i))),
        )

    def out_partner(h):
        return remote(psend.at[h], precv.at[h], p_s.at[h], p_r.at[h], (s, ring(t + inward(0))))

    def wait_arrival(i, o, h):
        q_arrival(i, o, h).wait_recv()

    started = []

    def go(copy):
        copy.start()
        started.append(copy)

    for h in range(1):
        go(q_partner(h))
        go(q_outward(0, 0, h))
    for i in range(REACH + 1, SIDE):
        for copy in kv_copies(i):
            go(copy)
    for h in range(1, 2):
        go(q_partner(h))
        go(q_outward(0, 0, h))

    loads[3].wait()
    loads[4].wait()
    nvt = nv[...].T
    lane = lax.broadcasted_iota(jnp.int32, (NEW, QROWS), 1)
    key_row = lax.broadcasted_iota(jnp.int32, (NEW, QROWS), 0)
    in_half = lax.rem(lane, HALF)
    own = []
    for h in range(2):
        row_id = jnp.where(
            in_half < BLK, order[h][0] * BLK + in_half, order[h][1] * BLK + in_half - BLK
        )
        own.append(attend(nk[...], nvt, qbuf[0, 0, h], key_row <= row_id))
    for i in range(REACH + 1):
        vt[i] = cv[:, columns(i)].T

    position = lax.broadcasted_iota(jnp.int32, (2 * N_CTX * 8, 2 * QROWS), 0)

    def keep(i, h, state):
        acc_ref[i, h] = state[0]
        stat_ref[i, h, 0:1, :] = state[1]
        stat_ref[i, h, 1:2, :] = state[2]

    def held(i, h):
        return acc_ref[i, h], stat_ref[i, h, 0:1, :], stat_ref[i, h, 1:2, :]

    def queries(i, h):
        return jnp.concatenate([qbuf[i, 0, h], qbuf[i, 1, h]], axis=0)

    def own_block(i, h):
        allowed = position < length - t * 256
        keep(i, h, attend(ck[:, columns(i)], vt[i], queries(i, h), allowed))

    def arrive(step, h):
        for i in range(REACH + 1):
            o = step - i
            if o in (0, 1) and (i, o) != (0, 0):
                wait_arrival(i, o, h)
                if i < REACH:
                    go(q_outward(i, o, h))

    for step in range(1, REACH + 2):
        for h in range(2):
            arrive(step, h)
            own_block(step - 1, h)

    for i in range(REACH + 1, SIDE):
        slot = i - REACH - 1
        for copy in kv_copies(i):
            copy.wait_recv()
        source = ring(t - inward(REACH) * (slot + 1))
        far_vt = vbuf[slot].T
        for h in range(2):
            allowed = position < length - source * 256
            part = attend(kbuf[slot], far_vt, queries(REACH, h), allowed)
            keep(REACH, h, merge(held(REACH, h), part))

    for i in range(REACH, 0, -1):
        for h in range(2):
            state = held(i, h)
            if i < REACH:
                out_inward(i + 1, h).wait_recv()
                state = merge(state, unpack(orecv[i, h]))
            osend[i - 1, h, :HD, :] = state[0].astype(jnp.bfloat16)
            osend[i - 1, h, HD:PACK, :] = pack_rows(state[1], state[2])
            go(out_inward(i, h))
    mine = []
    for h in range(2):
        out_inward(1, h).wait_recv()
        acc, top, total = merge(held(0, h), unpack(orecv[0, h]))
        psend[h, :HD, :] = acc[:, QROWS:].astype(jnp.bfloat16)
        psend[h, HD:PACK, :] = pack_rows(top[:, QROWS:], total[:, QROWS:])
        go(out_partner(h))
        keep(0, h, (acc, top, total))

    def finish(h):
        out_partner(h).wait_recv()
        acc, top, total = held(0, h)
        state = merge((acc[:, :QROWS], top[:, :QROWS], total[:, :QROWS]), own[h])
        acc, top, total = merge(state, unpack(precv[h]))
        rows = (acc / total).T
        for n in range(4):
            for part in range(2):
                lo = n * HALF + part * BLK
                fin_f[2 * h + part, :, n * HD : (n + 1) * HD] = rows[lo : lo + BLK]

    finish(0)
    shifted = out_first > first
    run[:BLK, :] = jnp.where(shifted, fin_f[1], fin_f[0]).astype(jnp.bfloat16)
    run[BLK:, :] = fin_f[1].astype(jnp.bfloat16)

    def p1_copy(k):
        there = lax.rem(chip + k, CHIPS)
        piece = run.at[
            pl.ds(pl.multiple_of((there // 4) * 16, 16), 16), pl.ds(pl.multiple_of(lax.rem(there, 4) * HD, HD), HD)
        ]
        return remote(piece, p1.at[core * CHIPS + chip], p1_s.at[k], p1_r.at[k], (2 * there + core, t))

    def p1_arrival(k):
        here = lax.rem(chip + CHIPS - k, CHIPS)
        return remote(p1.at[core * CHIPS + here], p1.at[core * CHIPS + here], p1_s.at[k], p1_r.at[k], (2 * here + core, t))

    my_rows = pl.ds(pl.multiple_of((chip // 4) * 16, 16), 16)
    my_cols = pl.ds(pl.multiple_of(lax.rem(chip, 4) * HD, HD), HD)
    for k in range(1, CHIPS):
        go(p1_copy(k))
    p1[core * CHIPS + chip] = run[my_rows, my_cols]

    finish(1)
    row32 = lax.broadcasted_iota(jnp.int32, (BLK, 4 * HD), 0)
    for b in range(4):
        place = jnp.where(
            first == b, 0, jnp.where(first + 1 == b, 1, jnp.where(rest_a == b, 2, 3))
        )
        rows = fin_f[place]
        row = row32 + b * BLK
        retained = (row < count) & ((row < out_start) | (row >= out_start + out_span))
        mixed_ref[b * BLK : (b + 1) * BLK, :] = jnp.where(retained, rows, 0.0).astype(jnp.bfloat16)

    for k in range(1, CHIPS):
        p1_arrival(k).wait_recv()
    mine16 = p1.at[pl.ds(core * CHIPS, CHIPS)]
    other16 = p1.at[pl.ds((1 - core) * CHIPS, CHIPS)]
    go(remote(mine16, mine16, p2_s.at[0], p2_r.at[0], (sibling, t)))
    other = remote(other16, other16, p2_s.at[0], p2_r.at[0], (sibling, t))
    other.wait_recv()

    def p3_copy(k):
        there = lax.rem(chip + k, CHIPS)
        return remote(p3.at[k], host.at[my_rows, my_cols], p3_s.at[k], p3_r.at[k], (2 * there + core, t))

    def p3_arrival(k):
        here = lax.rem(chip + CHIPS - k, CHIPS)
        place = host.at[
            pl.ds(pl.multiple_of((here // 4) * 16, 16), 16), pl.ds(pl.multiple_of(lax.rem(here, 4) * HD, HD), HD)
        ]
        return remote(place, place, p3_s.at[k], p3_r.at[k], (2 * here + core, t))

    slots = [lax.rem(offloads_ref[i, 0], 2) * CHIPS + lax.div(offloads_ref[i, 0], 2) for i in range(RUNS)]
    for k in range(CHIPS):
        target = 2 * lax.rem(chip + k, CHIPS) + core
        source = jnp.int32(0)
        for i in range(RUNS):
            source += jnp.where(offloads_ref[i, 1] == target, slots[i], 0)
        piece = p1[source]
        if k == 0:
            host[my_rows, my_cols] = piece
        else:
            p3[k] = piece
            go(p3_copy(k))
    for k in range(1, CHIPS):
        p3_arrival(k).wait_recv()
    row64 = lax.broadcasted_iota(jnp.int32, (CAP, 4 * HD), 0)
    hosted_ref[...] = jnp.where(row64 < in_span, host[...].astype(jnp.float32), 0.0).astype(jnp.bfloat16)

    for copy in started:
        copy.wait_send()


def local(
    new_queries, new_keys, new_values, cache_keys, cache_values, new_counts, ctx_lengths, offloads
):
    bf16, f32 = jnp.bfloat16, jnp.float32
    dma = pltpu.SemaphoreType.DMA
    smem = pl.BlockSpec(memory_space=pltpu.SMEM)
    anywhere = pl.BlockSpec(memory_space=pl.ANY)
    vmem = pl.BlockSpec(memory_space=pltpu.VMEM)
    far = max(FAR, 1)
    return pl.pallas_call(
        kernel,
        name="attend_and_relocate",
        out_shape=(
            jax.ShapeDtypeStruct((NEW, 4 * HD), bf16),
            jax.ShapeDtypeStruct((CAP, 4 * HD), bf16),
        ),
        in_specs=[smem] * 3 + [anywhere] * 5,
        out_specs=(vmem, vmem),
        scratch_shapes=[
            pltpu.VMEM((4, BLK, 4 * HD), bf16),
            pltpu.VMEM((NEW, HD), bf16),
            pltpu.VMEM((NEW, HD), bf16),
            pltpu.VMEM((256, KV * HD), bf16),
            pltpu.VMEM((256, KV * HD), bf16),
            pltpu.VMEM((REACH + 1, HD, 256), bf16),
            pltpu.VMEM((REACH + 1, 2, 2, QROWS, HD), bf16),
            pltpu.VMEM((far, 256, HD), bf16),
            pltpu.VMEM((far, 256, HD), bf16),
            pltpu.VMEM((REACH + 1, 2, HD, 2 * QROWS), f32),
            pltpu.VMEM((REACH + 1, 2, 8, 2 * QROWS), f32),
            pltpu.VMEM((REACH, 2, PACK, 2 * QROWS), bf16),
            pltpu.VMEM((REACH, 2, PACK, 2 * QROWS), bf16),
            pltpu.VMEM((2, PACK, QROWS), bf16),
            pltpu.VMEM((2, PACK, QROWS), bf16),
            pltpu.VMEM((4, BLK, 4 * HD), f32),
            pltpu.VMEM((CAP, 4 * HD), bf16),
            pltpu.VMEM((2 * CHIPS, 16, HD), bf16),
            pltpu.VMEM((CHIPS, 16, HD), bf16),
            pltpu.VMEM((CAP, 4 * HD), bf16),
            dma((5,)),
            dma((2, far)),
            dma((2, far)),
            dma((REACH + 1, 3, 2)),
            dma((REACH + 1, 2, 2)),
            dma((REACH, 2)),
            dma((REACH, 2)),
            dma((2,)),
            dma((2,)),
            dma((CHIPS,)),
            dma((CHIPS,)),
            dma((1,)),
            dma((1,)),
            dma((CHIPS,)),
            dma((CHIPS,)),
        ],
        compiler_params=pltpu.CompilerParams(
            collective_id=0, has_side_effects=True, vmem_limit_bytes=48 * 1024 * 1024
        ),
    )(new_counts, ctx_lengths, offloads, new_queries.reshape(4, BLK, 4 * HD), new_keys, new_values, cache_keys, cache_values)


def solution(mesh):
    placed = (
        P("stream", "ctx"),
        P("stream", None),
        P("stream", None),
        P(("stream", "ctx"), None),
        P(("stream", "ctx"), None),
        P(),
        P(),
        P(),
    )
    return jax.shard_map(
        local,
        mesh=mesh,
        in_specs=placed,
        out_specs=(P("stream", "ctx"), P("stream", "ctx")),
        check_vma=False,
    )
```

```python
import functools
import math

import jax
import jax.numpy as jnp
from jax import lax
from jax.experimental import pallas as pl
from jax.experimental.pallas import tpu as pltpu
from jax.sharding import PartitionSpec as P

HEADS = 64
KV = 8
HD = 128
BLK = 32
NEW = 128
CAP = 64
RUNS = 8
N_CTX = 16
N_STREAM = 32
CHIPS = N_STREAM // 2
SIDE = N_CTX // 2
REACH = 1
FAR = SIDE - 1 - REACH
KV_TURN = (0, 1, 2, 3, 4, 5, 6, 7)
OFFSETS = sorted(
    ((dx, dy) for dx in range(4) for dy in range(4)),
    key=lambda d: -(min(d[0], 4 - d[0]) + min(d[1], 4 - d[1])),
)
OFFSETS = OFFSETS[-1:] + OFFSETS[:-1]
HALF = NEW // 2
QROWS = 4 * HALF
PACK = HD + 16

NEG = -(2.0**100)
LOG2_SCALE = math.log2(math.e) / math.sqrt(HD)
MESH = pl.DeviceIdType.MESH
FIRST_QUERIES = (0, 1)
SCHEDULE = (('arrive', 1, 0), ('arrive', 1, 1), ('own', 0, 0), ('own', 0, 1), ('arrive', 2, 0), ('arrive', 2, 1), ('own', 1, 0), ('own', 1, 1), ('far', 2, 0), ('far', 2, 1), ('far', 3, 0), ('far', 3, 1), ('far', 4, 0), ('far', 4, 1), ('far', 5, 0), ('far', 5, 1), ('far', 6, 0), ('far', 6, 1), ('far', 7, 0), ('out', 1, 0), ('far', 7, 1), ('out', 1, 1), ('pair', 0))
LATE = (('pair', 1),)


def merge(first, second):
    acc_a, max_a, tot_a = first
    acc_b, max_b, tot_b = second
    top = jnp.maximum(max_a, max_b)
    scale_a = jnp.exp2(max_a - top)
    scale_b = jnp.exp2(max_b - top)
    return (acc_a * scale_a + acc_b * scale_b, top, tot_a * scale_a + tot_b * scale_b)


def attend(keys, values_t, queries, allowed):
    scores = lax.dot_general(
        keys, queries, (((1,), (1,)), ((), ())), preferred_element_type=jnp.float32
    )
    scores = jnp.where(allowed, scores * LOG2_SCALE, NEG)
    top = jnp.max(scores, axis=0, keepdims=True).astype(jnp.bfloat16).astype(jnp.float32)
    weights = jnp.exp2(scores - top)
    total = jnp.sum(weights, axis=0, keepdims=True)
    acc = jnp.dot(values_t, weights.astype(jnp.bfloat16), preferred_element_type=jnp.float32)
    return acc, top, total


def pack_rows(top, total):
    high = total.astype(jnp.bfloat16).astype(jnp.float32)
    low = total - high
    width = top.shape[1]
    row = lax.broadcasted_iota(jnp.int32, (16, width), 0)
    rows = jnp.where(row == 0, top, jnp.where(row == 1, high, jnp.where(row == 2, low, 0.0)))
    return rows.astype(jnp.bfloat16)


def unpack(packed):
    stats = packed[HD:PACK, :].astype(jnp.float32)
    return packed[:HD, :].astype(jnp.float32), stats[0:1], stats[1:2] + stats[2:3]


def kernel(
    counts_ref, lengths_ref, offloads_ref,
    q_hbm, nk_hbm, nv_hbm, ck_hbm, cv_hbm,
    mixed_ref, hosted_ref,
    q_in, nk, nv, ck, cv, vt, qbuf, kbuf, vbuf, far_vt, acc_ref, stat_ref, osend, orecv, psend, precv,
    fin_f, run, p1, p3, host,
    in_sem, kv_s, kv_r, q_s, q_r, o_s, o_r, p_s, p_r, p1_s, p1_r, p2_s, p2_r, p3_s, p3_r,
):
    s = lax.axis_index("stream")
    t = lax.axis_index("ctx")
    core = lax.rem(s, 2)
    chip = s // 2
    side = 1 - 2 * lax.rem(t, 2)

    def ring(v):
        return lax.rem(v + 2 * N_CTX, N_CTX)

    def inward(i):
        return side * (1 - 2 * lax.rem(i, 2))

    def near(i):
        return ring(t + inward(i) * i)

    def head(i):
        return near(i) // 2

    def distance(j):
        left = lax.rem(2 * j - t + N_CTX, N_CTX)
        return jnp.where(left < SIDE, left, N_CTX - 1 - left)

    def columns(i):
        return pl.ds(pl.multiple_of(head(i) * HD, HD), HD)

    own_kv = pl.ds(pl.multiple_of((t // 2) * HD, HD), HD)
    loads = [
        pltpu.make_async_copy(q_hbm, q_in, in_sem.at[0]),
        pltpu.make_async_copy(ck_hbm, ck, in_sem.at[1]),
        pltpu.make_async_copy(cv_hbm, cv, in_sem.at[2]),
        pltpu.make_async_copy(nk_hbm.at[:, own_kv], nk, in_sem.at[3]),
        pltpu.make_async_copy(nv_hbm.at[:, own_kv], nv, in_sem.at[4]),
    ]
    barrier = pltpu.get_barrier_semaphore()
    reach = max(FAR, 1)
    greeted = 0
    for k in range(1, reach + 1):
        for sign in (1, -1):
            pl.semaphore_signal(barrier, inc=1, device_id=(s, ring(t + sign * k)), device_id_type=MESH)
            greeted += 1
    for k in range(1, CHIPS):
        peer = 2 * lax.rem(chip + k, CHIPS) + core
        pl.semaphore_signal(barrier, inc=1, device_id=(peer, t), device_id_type=MESH)
        greeted += 1
    sibling = s + 1 - 2 * core
    pl.semaphore_signal(barrier, inc=1, device_id=(sibling, t), device_id_type=MESH)
    greeted += 1
    for copy in loads:
        copy.start()

    out_first = jnp.int32(0)
    out_span = jnp.int32(0)
    in_span = jnp.int32(0)
    for i in range(RUNS):
        mine = offloads_ref[0, i] == s
        out_first += jnp.where(mine, offloads_ref[2, i], 0)
        out_span += jnp.where(mine, offloads_ref[3, i] * BLK, 0)
        in_span += jnp.where(offloads_ref[1, i] == s, offloads_ref[3, i] * BLK, 0)
    count = counts_ref[s]
    length = lengths_ref[s]
    first = jnp.minimum(out_first, 2)
    rest_a = jnp.where(first == 0, 2, 0)
    rest_b = jnp.where(first == 2, 1, 3)
    order = ((first, first + 1), (rest_a, rest_b))
    out_start = out_first * BLK

    loads[0].wait()
    for h in range(2):
        for part in range(2):
            rows = q_in[order[h][part]]
            for n in range(4):
                lo = n * HALF + part * BLK
                qbuf[0, 0, h, lo : lo + BLK, :] = rows[:, n * HD : (n + 1) * HD]
    loads[1].wait()
    loads[2].wait()
    pl.semaphore_wait(barrier, greeted)

    def remote(src, dst, send, recv, device):
        return pltpu.make_async_remote_copy(
            src_ref=src, dst_ref=dst, send_sem=send, recv_sem=recv, device_id=device, device_id_type=MESH
        )

    def kv_copies(i):
        target = (s, ring(t + inward(i) * (i - REACH)))
        slot = i - REACH - 1
        return (
            remote(ck.at[:, columns(i)], kbuf.at[slot], kv_s.at[0, slot], kv_r.at[0, slot], target),
            remote(cv.at[:, columns(i)], vbuf.at[slot], kv_s.at[1, slot], kv_r.at[1, slot], target),
        )

    def q_partner(h):
        return remote(
            qbuf.at[0, 0, h], qbuf.at[0, 1, h], q_s.at[0, 2, h], q_r.at[0, 1, h], (s, ring(t + inward(0)))
        )

    def q_outward(i, o, h):
        return remote(
            qbuf.at[i, o, h], qbuf.at[i + 1, o, h], q_s.at[i, o, h], q_r.at[i + 1, o, h],
            (s, ring(t - inward(i))),
        )

    def q_arrival(i, o, h):
        return q_partner(h) if i == 0 else q_outward(i - 1, o, h)

    def out_inward(i, h, o):
        return remote(
            osend.at[i - 1, h, o], orecv.at[i - 1, h, o], o_s.at[i - 1, h, o], o_r.at[i - 1, h, o],
            (s, ring(t + inward(i))),
        )

    def out_partner(h):
        return remote(psend.at[h], precv.at[h], p_s.at[h], p_r.at[h], (s, ring(t + inward(0))))

    def wait_arrival(i, o, h):
        q_arrival(i, o, h).wait_recv()

    started = []

    def go(copy):
        copy.start()
        started.append(copy)

    def send_kv():
        for j in KV_TURN:
            i = distance(j)

            @pl.when(i > REACH)
            def _():
                for copy in kv_copies(i):
                    copy.start()

    def send_queries(h):
        go(q_partner(h))
        go(q_outward(0, 0, h))

    for h in FIRST_QUERIES:
        send_queries(h)
    send_kv()

    loads[3].wait()
    loads[4].wait()
    nvt = nv[...].T
    lane = lax.broadcasted_iota(jnp.int32, (NEW, QROWS), 1)
    key_row = lax.broadcasted_iota(jnp.int32, (NEW, QROWS), 0)
    in_half = lax.rem(lane, HALF)
    own = []
    for h in range(2):
        row_id = jnp.where(
            in_half < BLK, order[h][0] * BLK + in_half, order[h][1] * BLK + in_half - BLK
        )
        own.append(attend(nk[...], nvt, qbuf[0, 0, h], key_row <= row_id))
    for i in range(REACH + 1):
        vt[i] = cv[:, columns(i)].T

    position = lax.broadcasted_iota(jnp.int32, (2 * N_CTX * 8, 2 * QROWS), 0)

    def keep(i, h, state):
        for o in range(2):
            lo, hi = o * QROWS, (o + 1) * QROWS
            acc_ref[i, h, o] = state[0][:, lo:hi]
            stat_ref[i, h, o, 0:1, :] = state[1][:, lo:hi]
            stat_ref[i, h, o, 1:2, :] = state[2][:, lo:hi]

    def held(i, h, o):
        return acc_ref[i, h, o], stat_ref[i, h, o, 0:1, :], stat_ref[i, h, o, 1:2, :]

    def held_both(i, h):
        return tuple(jnp.concatenate(both, axis=1) for both in zip(held(i, h, 0), held(i, h, 1)))

    def queries(i, h):
        return jnp.concatenate([qbuf[i, 0, h], qbuf[i, 1, h]], axis=0)

    def own_block(i, h):
        allowed = position < length - t * 256
        keep(i, h, attend(ck[:, columns(i)], vt[i], queries(i, h), allowed))

    def arrive(step, h):
        for i in range(REACH + 1):
            o = step - i
            if o in (0, 1) and (i, o) != (0, 0):
                wait_arrival(i, o, h)
                if i < REACH:
                    go(q_outward(i, o, h))

    def far_block(i, h):
        slot = i - REACH - 1
        if h == 0:
            for copy in kv_copies(i):
                copy.wait_recv()
            far_vt[slot] = vbuf[slot].T
        source = ring(t - inward(REACH) * (slot + 1))
        allowed = position < length - source * 256
        part = attend(kbuf[slot], far_vt[slot], queries(REACH, h), allowed)
        keep(REACH, h, merge(held_both(REACH, h), part))

    def packed(ref, state):
        ref[:HD, :] = state[0].astype(jnp.bfloat16)
        ref[HD:PACK, :] = pack_rows(state[1], state[2])

    def out(i, h):
        for o in (1, 0):
            state = held(i, h, o)
            if i < REACH:
                out_inward(i + 1, h, o).wait_recv()
                state = merge(state, unpack(orecv[i, h, o]))
            packed(osend.at[i - 1, h, o], state)
            go(out_inward(i, h, o))

    def pair(h):
        out_inward(1, h, 1).wait_recv()
        packed(psend.at[h], merge(held(0, h, 1), unpack(orecv[0, h, 1])))
        go(out_partner(h))
        out_inward(1, h, 0).wait_recv()
        own[h] = merge(merge(held(0, h, 0), own[h]), unpack(orecv[0, h, 0]))

    def finish(h):
        out_partner(h).wait_recv()
        acc, top, total = merge(own[h], unpack(precv[h]))
        rows = (acc / total).T
        for n in range(4):
            for part in range(2):
                lo = n * HALF + part * BLK
                fin_f[2 * h + part, :, n * HD : (n + 1) * HD] = rows[lo : lo + BLK]

    actions = {
        "queries": send_queries, "arrive": arrive, "own": own_block, "far": far_block, "out": out, "pair": pair,
    }
    for name, *which in SCHEDULE:
        actions[name](*which)
    finish(0)
    shifted = out_first > first
    run[:BLK, :] = jnp.where(shifted, fin_f[1], fin_f[0]).astype(jnp.bfloat16)
    run[BLK:, :] = fin_f[1].astype(jnp.bfloat16)

    def chip_at(k, sign):
        dx, dy = OFFSETS[k]
        return lax.rem(chip // 4 + 4 + sign * dx, 4) * 4 + lax.rem(lax.rem(chip, 4) + 4 + sign * dy, 4)

    def piece(ref, i):
        rows = pl.ds(pl.multiple_of((i // 4) * 16, 16), 16)
        return ref.at[rows, pl.ds(pl.multiple_of(lax.rem(i, 4) * HD, HD), HD)]

    def p1_copy(k):
        there = chip_at(k, 1)
        return remote(
            piece(run, there), p1.at[core * CHIPS + chip], p1_s.at[k], p1_r.at[k], (2 * there + core, t)
        )

    def p1_arrival(k):
        here = chip_at(k, -1)
        return remote(
            p1.at[core * CHIPS + here], p1.at[core * CHIPS + here], p1_s.at[k], p1_r.at[k], (2 * here + core, t)
        )

    my_rows = pl.ds(pl.multiple_of((chip // 4) * 16, 16), 16)
    my_cols = pl.ds(pl.multiple_of(lax.rem(chip, 4) * HD, HD), HD)
    for k in range(1, CHIPS):
        go(p1_copy(k))
    p1[core * CHIPS + chip] = run[my_rows, my_cols]

    for name, *which in LATE:
        actions[name](*which)
    slots = [lax.rem(offloads_ref[0, i], 2) * CHIPS + lax.div(offloads_ref[0, i], 2) for i in range(RUNS)]
    wanted = []
    for k in range(CHIPS):
        target = 2 * chip_at(k, 1) + core
        wanted.append(sum(jnp.where(offloads_ref[1, i] == target, slots[i], 0) for i in range(RUNS)))
    for k in range(1, CHIPS):
        p1_arrival(k).wait_recv()
    mine16 = p1.at[pl.ds(core * CHIPS, CHIPS)]
    other16 = p1.at[pl.ds((1 - core) * CHIPS, CHIPS)]
    go(remote(mine16, mine16, p2_s.at[0], p2_r.at[0], (sibling, t)))
    other = remote(other16, other16, p2_s.at[0], p2_r.at[0], (sibling, t))
    other.wait_recv()

    def p3_copy(k):
        there = chip_at(k, 1)
        return remote(p3.at[k], piece(host, chip), p3_s.at[k], p3_r.at[k], (2 * there + core, t))

    def p3_arrival(k):
        here = chip_at(k, -1)
        return remote(piece(host, here), piece(host, here), p3_s.at[k], p3_r.at[k], (2 * here + core, t))

    for k in range(1, CHIPS):
        p3[k] = p1[wanted[k]]
        go(p3_copy(k))
    host[my_rows, my_cols] = p1[wanted[0]]
    finish(1)
    row32 = lax.broadcasted_iota(jnp.int32, (BLK, 4 * HD), 0)
    for b in range(4):
        place = jnp.where(
            first == b, 0, jnp.where(first + 1 == b, 1, jnp.where(rest_a == b, 2, 3))
        )
        rows = fin_f[place]
        row = row32 + b * BLK
        retained = (row < count) & ((row < out_start) | (row >= out_start + out_span))
        mixed_ref[b * BLK : (b + 1) * BLK, :] = jnp.where(retained, rows, 0.0).astype(jnp.bfloat16)

    passed = started[-(CHIPS - 1) :]
    for copy in started[: -(CHIPS - 1)]:
        copy.wait_send()
    for i in range(REACH + 1, SIDE):
        for copy in kv_copies(i):
            copy.wait_send()
    for k in range(1, CHIPS):
        p3_arrival(k).wait_recv()
    row64 = lax.broadcasted_iota(jnp.int32, (CAP, 4 * HD), 0)
    hosted_ref[...] = jnp.where(row64 < in_span, host[...].astype(jnp.float32), 0.0).astype(jnp.bfloat16)

    for copy in passed:
        copy.wait_send()


def local(
    new_queries, new_keys, new_values, cache_keys, cache_values, new_counts, ctx_lengths, offloads
):
    bf16, f32 = jnp.bfloat16, jnp.float32
    dma = pltpu.SemaphoreType.DMA
    smem = pl.BlockSpec(memory_space=pltpu.SMEM)
    anywhere = pl.BlockSpec(memory_space=pl.ANY)
    vmem = pl.BlockSpec(memory_space=pltpu.VMEM)
    far = max(FAR, 1)
    return pl.pallas_call(
        kernel,
        name="attend_and_relocate",
        out_shape=(
            jax.ShapeDtypeStruct((NEW, 4 * HD), bf16),
            jax.ShapeDtypeStruct((CAP, 4 * HD), bf16),
        ),
        in_specs=[smem] * 3 + [anywhere] * 5,
        out_specs=(vmem, vmem),
        scratch_shapes=[
            pltpu.VMEM((4, BLK, 4 * HD), bf16),
            pltpu.VMEM((NEW, HD), bf16),
            pltpu.VMEM((NEW, HD), bf16),
            pltpu.VMEM((256, KV * HD), bf16),
            pltpu.VMEM((256, KV * HD), bf16),
            pltpu.VMEM((REACH + 1, HD, 256), bf16),
            pltpu.VMEM((REACH + 1, 2, 2, QROWS, HD), bf16),
            pltpu.VMEM((far, 256, HD), bf16),
            pltpu.VMEM((far, 256, HD), bf16),
            pltpu.VMEM((far, HD, 256), bf16),
            pltpu.VMEM((REACH + 1, 2, 2, HD, QROWS), f32),
            pltpu.VMEM((REACH + 1, 2, 2, 8, QROWS), f32),
            pltpu.VMEM((REACH, 2, 2, PACK, QROWS), bf16),
            pltpu.VMEM((REACH, 2, 2, PACK, QROWS), bf16),
            pltpu.VMEM((2, PACK, QROWS), bf16),
            pltpu.VMEM((2, PACK, QROWS), bf16),
            pltpu.VMEM((4, BLK, 4 * HD), f32),
            pltpu.VMEM((CAP, 4 * HD), bf16),
            pltpu.VMEM((2 * CHIPS, 16, HD), bf16),
            pltpu.VMEM((CHIPS, 16, HD), bf16),
            pltpu.VMEM((CAP, 4 * HD), bf16),
            dma((5,)),
            dma((2, far)),
            dma((2, far)),
            dma((REACH + 1, 3, 2)),
            dma((REACH + 1, 2, 2)),
            dma((REACH, 2, 2)),
            dma((REACH, 2, 2)),
            dma((2,)),
            dma((2,)),
            dma((CHIPS,)),
            dma((CHIPS,)),
            dma((1,)),
            dma((1,)),
            dma((CHIPS,)),
            dma((CHIPS,)),
        ],
        compiler_params=pltpu.CompilerParams(
            collective_id=0, has_side_effects=True, vmem_limit_bytes=60 * 1024 * 1024
        ),
    )(new_counts, ctx_lengths, offloads.T, new_queries.reshape(4, BLK, 4 * HD), new_keys, new_values, cache_keys, cache_values)


def solution(mesh):
    placed = (
        P("stream", "ctx"),
        P("stream", None),
        P("stream", None),
        P(("stream", "ctx"), None),
        P(("stream", "ctx"), None),
        P(),
        P(),
        P(),
    )
    return jax.shard_map(
        local,
        mesh=mesh,
        in_specs=placed,
        out_specs=(P("stream", "ctx"), P("stream", "ctx")),
        check_vma=False,
    )
```

```python
import functools
import math

import jax
import jax.numpy as jnp
from jax import lax
from jax.experimental import pallas as pl
from jax.experimental.pallas import tpu as pltpu
from jax.sharding import PartitionSpec as P

HEADS = 64
KV = 8
HD = 128
BLK = 32
NEW = 128
CAP = 64
RUNS = 8
N_CTX = 16
N_STREAM = 32
CHIPS = N_STREAM // 2
SIDE = N_CTX // 2
REACH = 1
FAR = SIDE - 1 - REACH
KV_TURN = ((0, 1, 7, 2, 3, 4, 5, 6),)
OFFSETS = sorted(
    ((dx, dy) for dx in range(4) for dy in range(4)),
    key=lambda d: -(min(d[0], 4 - d[0]) + min(d[1], 4 - d[1])),
)
OFFSETS = OFFSETS[-1:] + OFFSETS[:-1]
HALF = NEW // 2
QROWS = 4 * HALF
PACK = HD + 16

NEG = -(2.0**100)
LOG2_SCALE = math.log2(math.e) / math.sqrt(HD)
MESH = pl.DeviceIdType.MESH
FIRST_QUERIES = (0, 1)
SCHEDULE = (('arrive', 1, 0), ('arrive', 1, 1), ('own', 0, 0), ('own', 0, 1), ('arrive', 2, 0), ('arrive', 2, 1), ('own', 1, 0), ('own', 1, 1), ('far', 2, 0), ('far', 3, 0), ('far', 4, 0), ('far', 5, 0), ('far', 6, 0), ('far', 7, 0), ('out', 1, 0), ('far', 2, 1), ('far', 3, 1), ('far', 4, 1), ('far', 5, 1), ('far', 6, 1), ('far', 7, 1), ('out', 1, 1), ('pair', 0))
LATE = (('pair', 1),)


def merge(first, second):
    acc_a, max_a, tot_a = first
    acc_b, max_b, tot_b = second
    top = jnp.maximum(max_a, max_b)
    scale_a = jnp.exp2(max_a - top)
    scale_b = jnp.exp2(max_b - top)
    return (acc_a * scale_a + acc_b * scale_b, top, tot_a * scale_a + tot_b * scale_b)


def attend(keys, values_t, queries, allowed):
    scores = lax.dot_general(
        keys, queries, (((1,), (1,)), ((), ())), preferred_element_type=jnp.float32
    )
    scores = jnp.where(allowed, scores * LOG2_SCALE, NEG)
    top = jnp.max(scores, axis=0, keepdims=True).astype(jnp.bfloat16).astype(jnp.float32)
    weights = jnp.exp2(scores - top)
    total = jnp.sum(weights, axis=0, keepdims=True)
    acc = jnp.dot(values_t, weights.astype(jnp.bfloat16), preferred_element_type=jnp.float32)
    return acc, top, total


def pack_rows(top, total):
    high = total.astype(jnp.bfloat16).astype(jnp.float32)
    low = total - high
    width = top.shape[1]
    row = lax.broadcasted_iota(jnp.int32, (16, width), 0)
    rows = jnp.where(row == 0, top, jnp.where(row == 1, high, jnp.where(row == 2, low, 0.0)))
    return rows.astype(jnp.bfloat16)


def unpack(packed):
    stats = packed[HD:PACK, :].astype(jnp.float32)
    return packed[:HD, :].astype(jnp.float32), stats[0:1], stats[1:2] + stats[2:3]


def kernel(
    counts_ref, lengths_ref, offloads_ref,
    q_hbm, nk_hbm, nv_hbm, ck_hbm, cv_hbm,
    mixed_ref, hosted_ref,
    q_in, nk, nv, ck, cv, vt, qbuf, kbuf, vbuf, far_vt, acc_ref, stat_ref, osend, orecv, psend, precv,
    fin_f, run, p1, p3, host,
    in_sem, kv_s, kv_r, q_s, q_r, o_s, o_r, p_s, p_r, p1_s, p1_r, p2_s, p2_r, p3_s, p3_r,
):
    s = lax.axis_index("stream")
    t = lax.axis_index("ctx")
    core = lax.rem(s, 2)
    chip = s // 2
    side = 1 - 2 * lax.rem(t, 2)

    def ring(v):
        return lax.rem(v + 2 * N_CTX, N_CTX)

    def inward(i):
        return side * (1 - 2 * lax.rem(i, 2))

    def near(i):
        return ring(t + inward(i) * i)

    def head(i):
        return near(i) // 2

    def distance(j):
        left = lax.rem(2 * j - t + N_CTX, N_CTX)
        return jnp.where(left < SIDE, left, N_CTX - 1 - left)

    def columns(i):
        return pl.ds(pl.multiple_of(head(i) * HD, HD), HD)

    own_kv = pl.ds(pl.multiple_of((t // 2) * HD, HD), HD)
    loads = [
        pltpu.make_async_copy(q_hbm, q_in, in_sem.at[0]),
        pltpu.make_async_copy(ck_hbm, ck, in_sem.at[1]),
        pltpu.make_async_copy(cv_hbm, cv, in_sem.at[2]),
        pltpu.make_async_copy(nk_hbm.at[:, own_kv], nk, in_sem.at[3]),
        pltpu.make_async_copy(nv_hbm.at[:, own_kv], nv, in_sem.at[4]),
    ]
    barrier = pltpu.get_barrier_semaphore()
    reach = max(FAR, 1)
    greeted = 0
    for k in range(1, reach + 1):
        for sign in (1, -1):
            pl.semaphore_signal(barrier, inc=1, device_id=(s, ring(t + sign * k)), device_id_type=MESH)
            greeted += 1
    for k in range(1, CHIPS):
        peer = 2 * lax.rem(chip + k, CHIPS) + core
        pl.semaphore_signal(barrier, inc=1, device_id=(peer, t), device_id_type=MESH)
        greeted += 1
    sibling = s + 1 - 2 * core
    pl.semaphore_signal(barrier, inc=1, device_id=(sibling, t), device_id_type=MESH)
    greeted += 1
    for copy in loads:
        copy.start()

    out_first = jnp.int32(0)
    out_span = jnp.int32(0)
    in_span = jnp.int32(0)
    for i in range(RUNS):
        mine = offloads_ref[0, i] == s
        out_first += jnp.where(mine, offloads_ref[2, i], 0)
        out_span += jnp.where(mine, offloads_ref[3, i] * BLK, 0)
        in_span += jnp.where(offloads_ref[1, i] == s, offloads_ref[3, i] * BLK, 0)
    count = counts_ref[s]
    length = lengths_ref[s]
    first = jnp.minimum(out_first, 2)
    rest_a = jnp.where(first == 0, 2, 0)
    rest_b = jnp.where(first == 2, 1, 3)
    order = ((first, first + 1), (rest_a, rest_b))
    out_start = out_first * BLK

    loads[0].wait()
    for h in range(2):
        for part in range(2):
            rows = q_in[order[h][part]]
            for n in range(4):
                lo = n * HALF + part * BLK
                qbuf[0, 0, h, lo : lo + BLK, :] = rows[:, n * HD : (n + 1) * HD]
    loads[1].wait()
    loads[2].wait()
    pl.semaphore_wait(barrier, greeted)

    def remote(src, dst, send, recv, device):
        return pltpu.make_async_remote_copy(
            src_ref=src, dst_ref=dst, send_sem=send, recv_sem=recv, device_id=device, device_id_type=MESH
        )

    def kv_copies(i):
        target = (s, ring(t + inward(i) * (i - REACH)))
        slot = i - REACH - 1
        return (
            remote(ck.at[:, columns(i)], kbuf.at[slot], kv_s.at[0, slot], kv_r.at[0, slot], target),
            remote(cv.at[:, columns(i)], vbuf.at[slot], kv_s.at[1, slot], kv_r.at[1, slot], target),
        )

    def q_partner(h):
        return remote(
            qbuf.at[0, 0, h], qbuf.at[0, 1, h], q_s.at[0, 2, h], q_r.at[0, 1, h], (s, ring(t + inward(0)))
        )

    def q_outward(i, o, h):
        return remote(
            qbuf.at[i, o, h], qbuf.at[i + 1, o, h], q_s.at[i, o, h], q_r.at[i + 1, o, h],
            (s, ring(t - inward(i))),
        )

    def q_arrival(i, o, h):
        return q_partner(h) if i == 0 else q_outward(i - 1, o, h)

    def out_inward(i, h, o):
        return remote(
            osend.at[i - 1, h, o], orecv.at[i - 1, h, o], o_s.at[i - 1, h, o], o_r.at[i - 1, h, o],
            (s, ring(t + inward(i))),
        )

    def out_partner(h):
        return remote(psend.at[h], precv.at[h], p_s.at[h], p_r.at[h], (s, ring(t + inward(0))))

    def wait_arrival(i, o, h):
        q_arrival(i, o, h).wait_recv()

    started = []

    def go(copy):
        copy.start()
        started.append(copy)

    def send_kv(turn):
        for j in KV_TURN[turn]:
            i = distance(j)

            @pl.when(i > REACH)
            def _():
                for copy in kv_copies(i):
                    copy.start()

    def send_queries(h):
        go(q_partner(h))
        go(q_outward(0, 0, h))

    for h in FIRST_QUERIES:
        send_queries(h)
    send_kv(0)

    loads[3].wait()
    loads[4].wait()
    nvt = nv[...].T
    lane = lax.broadcasted_iota(jnp.int32, (NEW, QROWS), 1)
    key_row = lax.broadcasted_iota(jnp.int32, (NEW, QROWS), 0)
    in_half = lax.rem(lane, HALF)
    own = []
    for h in range(2):
        row_id = jnp.where(
            in_half < BLK, order[h][0] * BLK + in_half, order[h][1] * BLK + in_half - BLK
        )
        own.append(attend(nk[...], nvt, qbuf[0, 0, h], key_row <= row_id))
    for i in range(REACH + 1):
        vt[i] = cv[:, columns(i)].T

    position = lax.broadcasted_iota(jnp.int32, (2 * N_CTX * 8, 2 * QROWS), 0)

    def keep(i, h, state):
        for o in range(2):
            lo, hi = o * QROWS, (o + 1) * QROWS
            acc_ref[i, h, o] = state[0][:, lo:hi]
            stat_ref[i, h, o, 0:1, :] = state[1][:, lo:hi]
            stat_ref[i, h, o, 1:2, :] = state[2][:, lo:hi]

    def held(i, h, o):
        return acc_ref[i, h, o], stat_ref[i, h, o, 0:1, :], stat_ref[i, h, o, 1:2, :]

    def held_both(i, h):
        return tuple(jnp.concatenate(both, axis=1) for both in zip(held(i, h, 0), held(i, h, 1)))

    def queries(i, h):
        return jnp.concatenate([qbuf[i, 0, h], qbuf[i, 1, h]], axis=0)

    def own_block(i, h):
        allowed = position < length - t * 256
        keep(i, h, attend(ck[:, columns(i)], vt[i], queries(i, h), allowed))

    def arrive(step, h):
        for i in range(REACH + 1):
            o = step - i
            if o in (0, 1) and (i, o) != (0, 0):
                wait_arrival(i, o, h)
                if i < REACH:
                    go(q_outward(i, o, h))

    def far_block(i, h):
        slot = i - REACH - 1
        if h == 0:
            for copy in kv_copies(i):
                copy.wait_recv()
            far_vt[slot] = vbuf[slot].T
        source = ring(t - inward(REACH) * (slot + 1))
        allowed = position < length - source * 256
        part = attend(kbuf[slot], far_vt[slot], queries(REACH, h), allowed)
        keep(REACH, h, merge(held_both(REACH, h), part))

    def packed(ref, state):
        ref[:HD, :] = state[0].astype(jnp.bfloat16)
        ref[HD:PACK, :] = pack_rows(state[1], state[2])

    def out(i, h):
        for o in (1, 0):
            state = held(i, h, o)
            if i < REACH:
                out_inward(i + 1, h, o).wait_recv()
                state = merge(state, unpack(orecv[i, h, o]))
            packed(osend.at[i - 1, h, o], state)
            go(out_inward(i, h, o))

    def pair(h):
        out_inward(1, h, 1).wait_recv()
        packed(psend.at[h], merge(held(0, h, 1), unpack(orecv[0, h, 1])))
        go(out_partner(h))
        out_inward(1, h, 0).wait_recv()
        own[h] = merge(merge(held(0, h, 0), own[h]), unpack(orecv[0, h, 0]))

    def finish(h):
        out_partner(h).wait_recv()
        acc, top, total = merge(own[h], unpack(precv[h]))
        rows = (acc / total).T
        for n in range(4):
            for part in range(2):
                lo = n * HALF + part * BLK
                fin_f[2 * h + part, :, n * HD : (n + 1) * HD] = rows[lo : lo + BLK]

    actions = {
        "queries": send_queries, "kv": send_kv, "arrive": arrive, "own": own_block, "far": far_block, "out": out, "pair": pair,
    }
    for name, *which in SCHEDULE:
        actions[name](*which)
    finish(0)
    shifted = out_first > first
    run[:BLK, :] = jnp.where(shifted, fin_f[1], fin_f[0]).astype(jnp.bfloat16)
    run[BLK:, :] = fin_f[1].astype(jnp.bfloat16)

    def chip_at(k, sign):
        dx, dy = OFFSETS[k]
        return lax.rem(chip // 4 + 4 + sign * dx, 4) * 4 + lax.rem(lax.rem(chip, 4) + 4 + sign * dy, 4)

    def piece(ref, i):
        rows = pl.ds(pl.multiple_of((i // 4) * 16, 16), 16)
        return ref.at[rows, pl.ds(pl.multiple_of(lax.rem(i, 4) * HD, HD), HD)]

    def p1_copy(k):
        there = chip_at(k, 1)
        return remote(
            piece(run, there), p1.at[core * CHIPS + chip], p1_s.at[k], p1_r.at[k], (2 * there + core, t)
        )

    def p1_arrival(k):
        here = chip_at(k, -1)
        return remote(
            p1.at[core * CHIPS + here], p1.at[core * CHIPS + here], p1_s.at[k], p1_r.at[k], (2 * here + core, t)
        )

    my_rows = pl.ds(pl.multiple_of((chip // 4) * 16, 16), 16)
    my_cols = pl.ds(pl.multiple_of(lax.rem(chip, 4) * HD, HD), HD)
    for k in range(1, CHIPS):
        go(p1_copy(k))
    p1[core * CHIPS + chip] = run[my_rows, my_cols]

    for name, *which in LATE:
        actions[name](*which)
    slots = [lax.rem(offloads_ref[0, i], 2) * CHIPS + lax.div(offloads_ref[0, i], 2) for i in range(RUNS)]
    wanted = []
    for k in range(CHIPS):
        target = 2 * chip_at(k, 1) + core
        wanted.append(sum(jnp.where(offloads_ref[1, i] == target, slots[i], 0) for i in range(RUNS)))
    for k in range(1, CHIPS):
        p1_arrival(k).wait_recv()
    mine16 = p1.at[pl.ds(core * CHIPS, CHIPS)]
    other16 = p1.at[pl.ds((1 - core) * CHIPS, CHIPS)]
    go(remote(mine16, mine16, p2_s.at[0], p2_r.at[0], (sibling, t)))
    other = remote(other16, other16, p2_s.at[0], p2_r.at[0], (sibling, t))
    other.wait_recv()

    def p3_copy(k):
        there = chip_at(k, 1)
        return remote(p3.at[k], piece(host, chip), p3_s.at[k], p3_r.at[k], (2 * there + core, t))

    def p3_arrival(k):
        here = chip_at(k, -1)
        return remote(piece(host, here), piece(host, here), p3_s.at[k], p3_r.at[k], (2 * here + core, t))

    for k in range(1, CHIPS):
        p3[k] = p1[wanted[k]]
        go(p3_copy(k))
    host[my_rows, my_cols] = p1[wanted[0]]
    finish(1)
    row32 = lax.broadcasted_iota(jnp.int32, (BLK, 4 * HD), 0)
    for b in range(4):
        place = jnp.where(
            first == b, 0, jnp.where(first + 1 == b, 1, jnp.where(rest_a == b, 2, 3))
        )
        rows = fin_f[place]
        row = row32 + b * BLK
        retained = (row < count) & ((row < out_start) | (row >= out_start + out_span))
        mixed_ref[b * BLK : (b + 1) * BLK, :] = jnp.where(retained, rows, 0.0).astype(jnp.bfloat16)

    passed = started[-(CHIPS - 1) :]
    for copy in started[: -(CHIPS - 1)]:
        copy.wait_send()
    for i in range(REACH + 1, SIDE):
        for copy in kv_copies(i):
            copy.wait_send()
    for k in range(1, CHIPS):
        p3_arrival(k).wait_recv()
    row64 = lax.broadcasted_iota(jnp.int32, (CAP, 4 * HD), 0)
    hosted_ref[...] = jnp.where(row64 < in_span, host[...].astype(jnp.float32), 0.0).astype(jnp.bfloat16)

    for copy in passed:
        copy.wait_send()


def local(
    new_queries, new_keys, new_values, cache_keys, cache_values, new_counts, ctx_lengths, offloads
):
    bf16, f32 = jnp.bfloat16, jnp.float32
    dma = pltpu.SemaphoreType.DMA
    smem = pl.BlockSpec(memory_space=pltpu.SMEM)
    anywhere = pl.BlockSpec(memory_space=pl.ANY)
    vmem = pl.BlockSpec(memory_space=pltpu.VMEM)
    far = max(FAR, 1)
    return pl.pallas_call(
        kernel,
        name="attend_and_relocate",
        out_shape=(
            jax.ShapeDtypeStruct((NEW, 4 * HD), bf16),
            jax.ShapeDtypeStruct((CAP, 4 * HD), bf16),
        ),
        in_specs=[smem] * 3 + [anywhere] * 5,
        out_specs=(vmem, vmem),
        scratch_shapes=[
            pltpu.VMEM((4, BLK, 4 * HD), bf16),
            pltpu.VMEM((NEW, HD), bf16),
            pltpu.VMEM((NEW, HD), bf16),
            pltpu.VMEM((256, KV * HD), bf16),
            pltpu.VMEM((256, KV * HD), bf16),
            pltpu.VMEM((REACH + 1, HD, 256), bf16),
            pltpu.VMEM((REACH + 1, 2, 2, QROWS, HD), bf16),
            pltpu.VMEM((far, 256, HD), bf16),
            pltpu.VMEM((far, 256, HD), bf16),
            pltpu.VMEM((far, HD, 256), bf16),
            pltpu.VMEM((REACH + 1, 2, 2, HD, QROWS), f32),
            pltpu.VMEM((REACH + 1, 2, 2, 8, QROWS), f32),
            pltpu.VMEM((REACH, 2, 2, PACK, QROWS), bf16),
            pltpu.VMEM((REACH, 2, 2, PACK, QROWS), bf16),
            pltpu.VMEM((2, PACK, QROWS), bf16),
            pltpu.VMEM((2, PACK, QROWS), bf16),
            pltpu.VMEM((4, BLK, 4 * HD), f32),
            pltpu.VMEM((CAP, 4 * HD), bf16),
            pltpu.VMEM((2 * CHIPS, 16, HD), bf16),
            pltpu.VMEM((CHIPS, 16, HD), bf16),
            pltpu.VMEM((CAP, 4 * HD), bf16),
            dma((5,)),
            dma((2, far)),
            dma((2, far)),
            dma((REACH + 1, 3, 2)),
            dma((REACH + 1, 2, 2)),
            dma((REACH, 2, 2)),
            dma((REACH, 2, 2)),
            dma((2,)),
            dma((2,)),
            dma((CHIPS,)),
            dma((CHIPS,)),
            dma((1,)),
            dma((1,)),
            dma((CHIPS,)),
            dma((CHIPS,)),
        ],
        compiler_params=pltpu.CompilerParams(
            collective_id=0, has_side_effects=True, vmem_limit_bytes=60 * 1024 * 1024
        ),
    )(new_counts, ctx_lengths, offloads.T, new_queries.reshape(4, BLK, 4 * HD), new_keys, new_values, cache_keys, cache_values)


def solution(mesh):
    placed = (
        P("stream", "ctx"),
        P("stream", None),
        P("stream", None),
        P(("stream", "ctx"), None),
        P(("stream", "ctx"), None),
        P(),
        P(),
        P(),
    )
    return jax.shard_map(
        local,
        mesh=mesh,
        in_specs=placed,
        out_specs=(P("stream", "ctx"), P("stream", "ctx")),
        check_vma=False,
    )
```
